32 devices in a mesh: groups: 2 (over y), ranks: 4 (over z), tensor: 4 (over x, core).
Axes of the slice: x: 2, y: 2, z: 4, core: 2. Of those that a mesh axis runs over, the one named last changes fastest.
Arguments:
- queries: bfloat16 [32, 8192], P(('groups', 'ranks'), 'tensor'), parts along dimension 0, may hold values from -180 to 180
- cache: bfloat16 [32, 2, 1024, 1024], P(('groups', 'ranks'), None, None, 'tensor'), parts along dimension 0, may hold values from -7 to 7
- pages: bfloat16 [256, 2, 128, 1024], P(('groups', 'ranks'), None, None, 'tensor'), parts along dimension 0, may hold values from -6 to 6
- page_owner: int32 [256], P('groups'), parts along dimension 0, may hold values from 0 to 3, as said below
- page_slot: int32 [256], P('groups'), parts along dimension 0, may hold values from 0 to 31, as said below
- lengths: int32 [32], P(('groups', 'ranks')), parts along dimension 0, may hold values from 2 to 1024, as said below
- out_weight: bfloat16 [8192, 8192], P('tensor', 'ranks'), may hold values from -0.0625 to 0.0625
Outputs:
- layer_out: bfloat16 [32, 8192], P(('groups', 'tensor'), 'ranks'), parts along dimension 0
The draws below stay inside these ranges and needn't reach their ends.
There are 2 independent parts, one for each index of `groups`. The reference program is written for one: setup_inputs(seed, part) draws one part's arguments, and reference() takes and returns one part's arrays. A program takes and returns all parts, laid end to end along the dimension named above; an argument that names none is the same for every part. Nothing has to cross between parts.
Inputs may be any that keep to these rules, and one draw needn't show every extreme that they name: `page_owner`: rows r * 32 to (r + 1) * 32 - 1 are the pages made on rank r; a rank sends either no page or exactly 8 pages to an owner, and every owner receives exactly 32 pages in all. `page_slot`: over the 32 pages that one owner receives, the slots are 0 to 31, each once. `lengths`: some sequence reaches 1024.
All inputs are finite; a program needn't handle non-finite values.
Results may differ from the reference program's by a relative error of at most 0.012.
Values may be sent and summed in bfloat16 or wider, within the bound.
A program may use at most 128 MiB of HBM per device.

```python
import jax
import jax.numpy as jnp
from jax import lax

D = 8192
HEADS = 64
KV_HEADS = 8
HEAD = 128
PAGE = 128
SEQ_DEV = 4
RES_TOK = 1024
NEWP = 8
NEW_DEV = 32
CAP = 8
N_RANKS = 4


def drawn_rows(key):
    row_count = SEQ_DEV * N_RANKS
    first_keys = jax.random.truncated_normal(jax.random.fold_in(key, 70), -6.0, 6.0, (row_count, KV_HEADS * HEAD), jnp.float32)
    return first_keys


def placement(key):
    rank_count = N_RANKS
    group_count = NEW_DEV // CAP
    owner_perm = jax.random.permutation(jax.random.fold_in(key, 50), rank_count)
    source_perm = jax.random.permutation(jax.random.fold_in(key, 51), rank_count)
    offsets = jax.random.permutation(jax.random.fold_in(key, 52), rank_count)[:group_count]
    page_order = jax.vmap(lambda subkey: jax.random.permutation(subkey, NEW_DEV))(jax.random.split(jax.random.fold_in(key, 53), rank_count))
    group_index = page_order // CAP
    within_group = page_order % CAP
    owner = owner_perm[(source_perm[:, None] + offsets[group_index]) % rank_count]
    slot_perm = jax.vmap(lambda subkey: jax.random.permutation(subkey, NEW_DEV))(jax.random.split(jax.random.fold_in(key, 54), rank_count))
    slot = slot_perm[owner, group_index * CAP + within_group]
    return (owner.reshape(-1).astype(jnp.int32), slot.reshape(-1).astype(jnp.int32))


def draw_cache(key, part):
    first_keys = drawn_rows(key)
    key = jax.random.fold_in(key, 1)
    row_count = SEQ_DEV * N_RANKS
    values = jax.random.truncated_normal(key, -6.0, 6.0, (row_count, 2, RES_TOK, KV_HEADS * HEAD), jnp.float32)
    values = values.at[:, 0, 0].set(first_keys)
    return values.astype(jnp.bfloat16)


def draw_queries(key, part):
    key = jax.random.fold_in(key, 2)
    row_count = SEQ_DEV * N_RANKS
    values = jax.random.truncated_normal(key, -6.0, 6.0, (row_count, HEADS * HEAD), jnp.float32)
    return values.astype(jnp.bfloat16)


def draw_page_owner(key, part):
    return placement(key)[0]


def draw_page_slot(key, part):
    return placement(key)[1]


def draw_lengths(key, part):
    key = jax.random.fold_in(key, 5)
    row_count = SEQ_DEV * N_RANKS
    first = jax.random.randint(jax.random.fold_in(key, 1), (row_count,), 2, RES_TOK + 1)
    second = jax.random.randint(jax.random.fold_in(key, 2), (row_count,), 2, RES_TOK + 1)
    third = jax.random.randint(jax.random.fold_in(key, 3), (row_count,), 2, RES_TOK + 1)
    shortest = jnp.minimum(jnp.minimum(first, second), third)
    longest_row = jax.random.randint(jax.random.fold_in(key, 4), (), 0, row_count)
    return shortest.at[longest_row].set(RES_TOK).astype(jnp.int32)


def levels(rng, extent, pieces, smallest, high):
    def one(dim, shards_of):
        heights = jax.random.uniform(jax.random.fold_in(jax.random.fold_in(rng, 6), dim), (shards_of,), jnp.float32, smallest / len(pieces), high / len(pieces))
        return jnp.repeat(jnp.exp(heights), extent[dim] // shards_of).reshape((-1,) + (1,) * (len(extent) - dim - 1))

    gain = one(*pieces[0])
    for cut in pieces[1:]:
        gain = gain * one(*cut)
    return gain


def bell_draw(stream_key, extent, deviation, reach, cuts=(), held_as=jnp.bfloat16):
    gain = levels(stream_key, extent, cuts, -0.22, 0.18) if cuts else 1.0
    drawn = jax.random.normal(stream_key, extent, jnp.float32) * deviation * gain
    return jnp.minimum(jnp.maximum(drawn, -reach), reach).astype(held_as)


def setup_inputs(seed: int = 0, part: int = 0) -> dict:
    keys = jax.random.split(jax.random.key(seed), 8)
    part_splits = jax.random.split(jax.random.fold_in(keys[7], part), 8)
    queries = draw_queries(jax.random.fold_in(jax.random.fold_in(keys[7], part), 71), part)
    cache = draw_cache(jax.random.fold_in(jax.random.fold_in(keys[7], part), 71), part)
    pages = bell_draw(part_splits[2], (N_RANKS * NEW_DEV, 2, PAGE, KV_HEADS * HEAD), 1.0, 6.0, ((0, 4), (3, 4)))
    page_owner = draw_page_owner(jax.random.fold_in(jax.random.fold_in(keys[7], part), 71), part)
    page_slot = draw_page_slot(jax.random.fold_in(jax.random.fold_in(keys[7], part), 71), part)
    lengths = draw_lengths(jax.random.fold_in(jax.random.fold_in(keys[7], part), 71), part)
    out_weight = bell_draw(keys[6], (HEADS * HEAD, D), (HEADS * HEAD) ** -0.5, 0.0625, ((0, 4), (1, 4)))
    return {"queries": queries, "cache": cache, "pages": pages, "page_owner": page_owner, "page_slot": page_slot, "lengths": lengths, "out_weight": out_weight}


def reference(queries, cache, pages, page_owner, page_slot, lengths, out_weight):
    row_count = queries.shape[0]
    feature_width = cache.shape[-1]
    sequence = (page_owner * SEQ_DEV + page_slot // NEWP).astype(jnp.int32)
    within = (page_slot % NEWP).astype(jnp.int32)
    fresh_pages = jnp.zeros((row_count, NEWP, 2, PAGE, feature_width), jnp.bfloat16).at[sequence, within].set(pages)
    fresh_pages = jnp.transpose(fresh_pages, (0, 2, 1, 3, 4)).reshape(row_count, 2, NEWP * PAGE, feature_width)
    group_size = HEADS // KV_HEADS

    def attend(inputs):
        query_row, resident, newer_kv, length = inputs
        key_rows = jnp.concatenate([resident[0], newer_kv[0]], 0).reshape(-1, KV_HEADS, HEAD).astype(jnp.float32)
        value_rows = jnp.concatenate([resident[1], newer_kv[1]], 0).reshape(-1, KV_HEADS, HEAD).astype(jnp.float32)
        query_grid = query_row.reshape(KV_HEADS, group_size, HEAD).astype(jnp.float32)
        scores = jnp.einsum("hgd,lhd->hgl", query_grid, key_rows) * (HEAD ** -0.5)
        position = jnp.arange(key_rows.shape[0])
        live_mask = (position < length) | (position >= RES_TOK)
        scores = jnp.where(live_mask[None, None, :], scores, -jnp.inf)
        row_peak = jnp.max(scores, axis=-1, keepdims=True)
        exp_scores = jnp.exp(scores - row_peak)
        row_total = jnp.sum(exp_scores, axis=-1, keepdims=True)
        weights = lax.optimization_barrier(exp_scores.astype(jnp.bfloat16)).astype(jnp.float32)
        mixture = jnp.einsum("hgl,lhd->hgd", weights, value_rows) / row_total
        return mixture.astype(jnp.bfloat16).reshape(-1)

    attended = lax.map(attend, (queries, cache, fresh_pages, lengths))
    return jnp.dot(attended, out_weight, preferred_element_type=jnp.float32).astype(jnp.bfloat16)
```

```python
import functools

import jax
import jax.numpy as jnp
from jax import lax
from jax.experimental import pallas as pl
from jax.experimental.pallas import tpu as pltpu
from jax.sharding import PartitionSpec as P

HEAD = 128
MESH = pl.DeviceIdType.MESH
LOWEST = -1e30
W_PARTS = 4
PAGE_PARTS = 4


def kernel(
    ranks,
    tensors,
    seq_ref,
    table_ref,
    length_ref,
    q_ref,
    cache_hbm,
    pages_hbm,
    weight_hbm,
    out_ref,
    cache_v,
    pages_v,
    weight_v,
    q_recv,
    q_wide,
    part_o,
    part_m,
    part_l,
    o_send,
    o_recv,
    ml_send,
    ml_recv,
    att_send,
    att_recv,
    att_f32,
    att_wide,
    terms,
    sum_send,
    sum_recv,
    load_sem,
    q_sems,
    o_sems,
    ml_sems,
    att_sems,
    sum_sems,
):
    me = lax.axis_index("ranks")
    my_tensor = lax.axis_index("tensor")
    seqs, heads, _ = q_ref.shape
    pages = pages_v.shape[0]
    per_seq = pages // seqs
    resident = cache_v.shape[2]
    half = heads // 2
    all_seqs = ranks * seqs
    scale = HEAD ** (-0.5)
    rows = seqs * heads

    loads = []
    for j in range(seqs):
        loads.append(pltpu.make_async_copy(cache_hbm.at[j], cache_v.at[j], load_sem.at[j]))
    step = pages // PAGE_PARTS
    for j in range(PAGE_PARTS):
        span = pl.ds(j * step, step)
        loads.append(
            pltpu.make_async_copy(pages_hbm.at[span], pages_v.at[span], load_sem.at[seqs + j])
        )
    depth = weight_v.shape[0] // W_PARTS
    for j in range(W_PARTS):
        span = pl.ds(j * depth, depth)
        loads.append(
            pltpu.make_async_copy(
                weight_hbm.at[span], weight_v.at[span], load_sem.at[seqs + PAGE_PARTS + j]
            )
        )
    for load in loads:
        load.start()

    barrier = pltpu.get_barrier_semaphore()
    for d in range(1, ranks):
        pl.semaphore_signal(
            barrier, inc=1, device_id={"ranks": lax.rem(me + d, ranks)}, device_id_type=MESH
        )
    for d in range(1, tensors):
        pl.semaphore_signal(
            barrier,
            inc=1,
            device_id={"tensor": lax.rem(my_tensor + d, tensors)},
            device_id_type=MESH,
        )
    pl.semaphore_wait(barrier, ranks + tensors - 2)

    def to_rank(d, source, target, sems):
        return pltpu.make_async_remote_copy(
            src_ref=source,
            dst_ref=target.at[d],
            send_sem=sems.at[0, d],
            recv_sem=sems.at[1, d],
            device_id={"ranks": lax.rem(me + d, ranks)},
            device_id_type=MESH,
        )

    q_copies = [to_rank(d, q_ref, q_recv, q_sems) for d in range(1, ranks)]
    for copy in q_copies:
        copy.start()

    upper = lax.broadcasted_iota(jnp.int32, (heads, HEAD), 0) < half

    def widen(q):
        wide = q.astype(jnp.float32)
        zero = jnp.zeros_like(wide)
        return jnp.concatenate(
            [jnp.where(upper, wide, zero), jnp.where(upper, zero, wide)], axis=1
        ).astype(jnp.bfloat16)

    def score(q, keys):
        return (
            lax.dot_general(q, keys, (((1,), (1,)), ((), ())), preferred_element_type=jnp.float32)
            * scale
        )

    def finish(scores, values, slot):
        peak = jnp.max(scores, axis=1, keepdims=True)
        exps = jnp.exp(scores - peak)
        total = jnp.sum(exps, axis=1, keepdims=True)
        mix = jnp.dot(exps.astype(jnp.bfloat16), values, preferred_element_type=jnp.float32)
        part_o[slot] = jnp.where(upper, mix[:, :HEAD], mix[:, HEAD:])
        part_m[slot] = jnp.broadcast_to(peak, (heads, HEAD))
        part_l[slot] = jnp.broadcast_to(total, (heads, HEAD))

    for j in range(seqs):
        q_wide[me * seqs + j] = widen(q_ref[j])
    part_o[pages] = jnp.zeros((heads, HEAD), jnp.float32)
    part_m[pages] = jnp.full((heads, HEAD), LOWEST, jnp.float32)
    part_l[pages] = jnp.zeros((heads, HEAD), jnp.float32)
    position = lax.broadcasted_iota(jnp.int32, (heads, resident), 1)
    for j in range(seqs):
        loads[j].wait()
        scores = score(q_wide[me * seqs + j], cache_v[j, 0])
        scores = jnp.where(position < length_ref[j], scores, -jnp.inf)
        finish(scores, cache_v[j, 1], pages + 1 + j)

    for d in range(1, ranks):
        q_copies[d - 1].wait_recv()
        source = lax.rem(me - d + ranks, ranks)
        for j in range(seqs):
            q_wide[source * seqs + j] = widen(q_recv[d, j])

    for j in range(PAGE_PARTS):
        loads[seqs + j].wait()

        for i in range(step):
            page = j * step + i
            finish(score(q_wide[seq_ref[page]], pages_v[page, 0]), pages_v[page, 1], page)

    lane = lax.broadcasted_iota(jnp.int32, (rows, HEAD), 1)
    row = lax.broadcasted_iota(jnp.int32, (rows, HEAD), 0)
    low_diagonal = lane == row
    high_diagonal = lane == row + rows

    def gather_owner(owner):
        peaks, totals, sums = [], [], []
        for j in range(seqs):
            slots = [table_ref[(owner * seqs + j) * per_seq + k] for k in range(per_seq)]
            slot_peaks = [part_m[slot] for slot in slots]
            peak = functools.reduce(jnp.maximum, slot_peaks)
            factors = [jnp.exp(one - peak) for one in slot_peaks]
            peaks.append(peak)
            totals.append(sum(f * part_l[slot] for f, slot in zip(factors, slots)))
            sums.append(sum(f * part_o[slot] for f, slot in zip(factors, slots)))
        return [jnp.concatenate(x, axis=0) for x in (peaks, totals, sums)]

    o_copies, ml_copies = [], []
    for d in range(1, ranks):
        peak, total, mix = gather_owner(lax.rem(me + d, ranks))
        o_send[d] = mix.astype(jnp.bfloat16)
        packed = jnp.where(low_diagonal, peak, jnp.where(high_diagonal, total, 0.0))
        ml_send[d] = jnp.broadcast_to(jnp.sum(packed, axis=0, keepdims=True), (8, HEAD))
        o_copies.append(to_rank(d, o_send.at[d], o_recv, o_sems))
        ml_copies.append(to_rank(d, ml_send.at[d], ml_recv, ml_sems))
        ml_copies[-1].start()
        o_copies[-1].start()

    peak, total, mix = gather_owner(me)
    own = pl.ds(pages + 1, seqs)
    states = [
        (peak, total, mix),
        tuple(x[own].reshape(rows, HEAD) for x in (part_m, part_l, part_o)),
    ]

    def merge(a, b):
        top = jnp.maximum(a[0], b[0])
        fa, fb = jnp.exp(a[0] - top), jnp.exp(b[0] - top)
        return top, fa * a[1] + fb * b[1], fa * a[2] + fb * b[2]

    state = merge(*states)
    for d in range(1, ranks):
        ml_copies[d - 1].wait_recv()
        o_copies[d - 1].wait_recv()
        spread = jnp.broadcast_to(ml_recv[d, 0:1, :], (rows, HEAD))
        peak = jnp.sum(jnp.where(low_diagonal, spread, 0.0), axis=1, keepdims=True)
        total = jnp.sum(jnp.where(high_diagonal, spread, 0.0), axis=1, keepdims=True)
        state = merge(
            state,
            (
                jnp.broadcast_to(peak, (rows, HEAD)),
                jnp.broadcast_to(total, (rows, HEAD)),
                o_recv[d].astype(jnp.float32),
            ),
        )
    attended = (state[2] / state[1]).astype(jnp.bfloat16)
    att_send[...] = attended
    att_copies = [to_rank(d, att_send, att_recv, att_sems) for d in range(1, ranks)]
    for copy in att_copies:
        copy.start()

    def place(source, value):
        att_f32[pl.ds(source * seqs, seqs)] = value.astype(jnp.float32).reshape(seqs, heads, HEAD)

    place(me, attended)
    for d in range(1, ranks):
        att_copies[d - 1].wait_recv()
        place(lax.rem(me - d + ranks, ranks), att_recv[d])
    for h in range(heads):
        att_wide[:, h * HEAD : (h + 1) * HEAD] = att_f32[:, h, :].astype(jnp.bfloat16)

    for j in range(W_PARTS):
        loads[seqs + PAGE_PARTS + j].wait()
    width = weight_v.shape[1]
    block = min(width, 256)
    share = all_seqs // tensors

    @pl.loop(0, width // block)
    def _(n):
        span = pl.ds(pl.multiple_of(n * block, block), block)
        product = jnp.dot(att_wide[...], weight_v[:, span], preferred_element_type=jnp.float32)
        for t in range(tensors):
            terms[t, :, span] = product[t * share : (t + 1) * share]

    _, sum_rows, sum_cols = sum_send.shape
    folds = sum_rows // share

    def fold(t):
        chunk = terms[t]
        return jnp.concatenate(
            [chunk[:, c * sum_cols : (c + 1) * sum_cols] for c in range(folds)], axis=0
        )

    sum_copies = []
    for d in range(1, tensors):
        target = lax.rem(my_tensor + d, tensors)
        sum_send[d] = fold(target).astype(jnp.bfloat16)
        copy = pltpu.make_async_remote_copy(
            src_ref=sum_send.at[d],
            dst_ref=sum_recv.at[d],
            send_sem=sum_sems.at[0, d],
            recv_sem=sum_sems.at[1, d],
            device_id={"tensor": target},
            device_id_type=MESH,
        )
        copy.start()
        sum_copies.append(copy)
    result = fold(my_tensor)
    for d in range(1, tensors):
        sum_copies[d - 1].wait_recv()
        result = result + sum_recv[d].astype(jnp.float32)
    for c in range(folds):
        out_ref[:, c * sum_cols : (c + 1) * sum_cols] = result[
            c * share : (c + 1) * share
        ].astype(jnp.bfloat16)

    for copy in q_copies + o_copies + ml_copies + att_copies + sum_copies:
        copy.wait_send()


def per_device(queries, cache, pages, page_owner, page_slot, lengths, out_weight):
    ranks = lax.axis_size("ranks")
    tensors = lax.axis_size("tensor")
    me = lax.axis_index("ranks")
    seqs, width = queries.shape
    heads = width // HEAD
    page_count = pages.shape[0]
    kv_width = cache.shape[-1]
    resident = cache.shape[2]
    features = out_weight.shape[1]
    own = me * page_count
    place = lax.dynamic_slice_in_dim(
        page_owner * page_count + page_slot, own, page_count, 0
    )
    seq_of_page = place // (page_count // seqs)
    match = jnp.arange(ranks * page_count)[:, None] == place[None, :]
    table = jnp.min(jnp.where(match, jnp.arange(page_count)[None, :], page_count), axis=1)
    all_seqs = ranks * seqs
    share = all_seqs // tensors
    folds = max(1, 16 // share)
    rows = seqs * heads
    slots = page_count + 1 + seqs
    bf16, f32 = jnp.bfloat16, jnp.float32
    smem = pl.BlockSpec(memory_space=pltpu.SMEM)
    vmem = pl.BlockSpec(memory_space=pltpu.VMEM)
    hbm = pl.BlockSpec(memory_space=pl.ANY)
    sems = pltpu.SemaphoreType.DMA
    return pl.pallas_call(
        functools.partial(kernel, ranks, tensors),
        out_shape=jax.ShapeDtypeStruct((share, features), bf16),
        in_specs=[smem, smem, smem, vmem, hbm, hbm, hbm],
        out_specs=vmem,
        scratch_shapes=[
            pltpu.VMEM(cache.shape, bf16),
            pltpu.VMEM(pages.shape, bf16),
            pltpu.VMEM(out_weight.shape, bf16),
            pltpu.VMEM((ranks, seqs, heads, HEAD), bf16),
            pltpu.VMEM((all_seqs, heads, kv_width), bf16),
            pltpu.VMEM((slots, heads, HEAD), f32),
            pltpu.VMEM((slots, heads, HEAD), f32),
            pltpu.VMEM((slots, heads, HEAD), f32),
            pltpu.VMEM((ranks, rows, HEAD), bf16),
            pltpu.VMEM((ranks, rows, HEAD), bf16),
            pltpu.VMEM((ranks, 8, HEAD), f32),
            pltpu.VMEM((ranks, 8, HEAD), f32),
            pltpu.VMEM((rows, HEAD), bf16),
            pltpu.VMEM((ranks, rows, HEAD), bf16),
            pltpu.VMEM((all_seqs, heads, HEAD), f32),
            pltpu.VMEM((all_seqs, width), bf16),
            pltpu.VMEM((tensors, share, features), f32),
            pltpu.VMEM((tensors, share * folds, features // folds), bf16),
            pltpu.VMEM((tensors, share * folds, features // folds), bf16),
            sems((seqs + PAGE_PARTS + W_PARTS,)),
            sems((2, ranks)),
            sems((2, ranks)),
            sems((2, ranks)),
            sems((2, ranks)),
            sems((2, tensors)),
        ],
        compiler_params=pltpu.CompilerParams(
            collective_id=0, has_side_effects=True, vmem_limit_bytes=48 * 1024 * 1024
        ),
        cost_estimate=pl.CostEstimate(
            flops=2 * all_seqs * width * features,
            bytes_accessed=2 * (cache.size + pages.size + out_weight.size),
            transcendentals=0,
        ),
    )(
        seq_of_page,
        table,
        lengths,
        queries.reshape(seqs, heads, HEAD),
        cache,
        pages,
        out_weight,
    )


def solution(mesh):
    placed = (
        P(("groups", "ranks"), "tensor"),
        P(("groups", "ranks"), None, None, "tensor"),
        P(("groups", "ranks"), None, None, "tensor"),
        P("groups"),
        P("groups"),
        P(("groups", "ranks")),
        P("tensor", "ranks"),
    )
    return jax.shard_map(
        per_device,
        mesh=mesh,
        in_specs=placed,
        out_specs=P(("groups", "tensor"), "ranks"),
        check_vma=False,
    )
```

```python
import functools

import jax
import jax.numpy as jnp
from jax import lax
from jax.experimental import pallas as pl
from jax.experimental.pallas import tpu as pltpu
from jax.sharding import PartitionSpec as P

HEAD = 128
MESH = pl.DeviceIdType.MESH
LOWEST = -1e30
W_PARTS = 4
PAGE_PARTS = 4


def kernel(
    ranks,
    tensors,
    owner_hbm,
    slot_hbm,
    length_hbm,
    query_ref,
    cache_hbm,
    pages_hbm,
    weight_hbm,
    out_ref,
    owner_ref,
    slot_ref,
    length_ref,
    table_v,
    table_ref,
    q_f32,
    q_ref,
    cache_v,
    pages_v,
    weight_v,
    q_recv,
    q_wide,
    part_o,
    part_m,
    part_l,
    o_send,
    o_recv,
    ml_send,
    ml_recv,
    att_send,
    att_recv,
    att_f32,
    att_wide,
    terms,
    sum_send,
    sum_recv,
    meta_sem,
    load_sem,
    q_sems,
    o_sems,
    ml_sems,
    att_sems,
    sum_sems,
):
    me = lax.axis_index("ranks")
    my_tensor = lax.axis_index("tensor")
    seqs, heads, _ = q_ref.shape
    pages = pages_v.shape[0]
    per_seq = pages // seqs
    resident = cache_v.shape[2]
    half = heads // 2
    all_seqs = ranks * seqs
    scale = HEAD ** (-0.5)
    rows = seqs * heads

    metas = [
        pltpu.make_async_copy(source, target, meta_sem.at[k])
        for k, (source, target) in enumerate(
            ((owner_hbm, owner_ref), (slot_hbm, slot_ref), (length_hbm, length_ref))
        )
    ]
    for copy in metas:
        copy.start()

    loads = []
    for j in range(seqs):
        loads.append(pltpu.make_async_copy(cache_hbm.at[j], cache_v.at[j], load_sem.at[j]))
    step = pages // PAGE_PARTS
    for j in range(PAGE_PARTS):
        span = pl.ds(j * step, step)
        loads.append(
            pltpu.make_async_copy(pages_hbm.at[span], pages_v.at[span], load_sem.at[seqs + j])
        )
    depth = weight_v.shape[0] // W_PARTS
    for j in range(W_PARTS):
        span = pl.ds(j * depth, depth)
        loads.append(
            pltpu.make_async_copy(
                weight_hbm.at[span], weight_v.at[span], load_sem.at[seqs + PAGE_PARTS + j]
            )
        )
    for load in loads[: seqs + PAGE_PARTS]:
        load.start()

    barrier = pltpu.get_barrier_semaphore()
    for d in range(1, ranks):
        pl.semaphore_signal(
            barrier, inc=1, device_id={"ranks": lax.rem(me + d, ranks)}, device_id_type=MESH
        )
    for d in range(1, tensors):
        pl.semaphore_signal(
            barrier,
            inc=1,
            device_id={"tensor": lax.rem(my_tensor + d, tensors)},
            device_id_type=MESH,
        )
    for h in range(heads):
        q_f32[:, h, :] = query_ref[:, h * HEAD : (h + 1) * HEAD].astype(jnp.float32)
    q_ref[...] = q_f32[...].astype(jnp.bfloat16)
    pl.semaphore_wait(barrier, ranks + tensors - 2)

    def to_rank(d, source, target, sems):
        return pltpu.make_async_remote_copy(
            src_ref=source,
            dst_ref=target.at[d],
            send_sem=sems.at[0, d],
            recv_sem=sems.at[1, d],
            device_id={"ranks": lax.rem(me + d, ranks)},
            device_id_type=MESH,
        )

    q_copies = [to_rank(d, q_ref, q_recv, q_sems) for d in range(1, ranks)]
    for copy in q_copies:
        copy.start()

    upper = lax.broadcasted_iota(jnp.int32, (heads, HEAD), 0) < half

    def widen(q):
        wide = q.astype(jnp.float32)
        zero = jnp.zeros_like(wide)
        return jnp.concatenate(
            [jnp.where(upper, wide, zero), jnp.where(upper, zero, wide)], axis=1
        ).astype(jnp.bfloat16)

    def score(q, keys):
        return (
            lax.dot_general(q, keys, (((1,), (1,)), ((), ())), preferred_element_type=jnp.float32)
            * scale
        )

    def parts(count, scores, values, first):
        block = jnp.concatenate(scores, axis=0)
        peak = jnp.max(block, axis=1, keepdims=True)
        exps = jnp.exp(block - peak)
        total = jnp.sum(exps, axis=1, keepdims=True)
        span = pl.ds(first, count)
        shape = (count, heads, HEAD)
        part_m[span] = jnp.broadcast_to(peak, (count * heads, HEAD)).reshape(shape)
        part_l[span] = jnp.broadcast_to(total, (count * heads, HEAD)).reshape(shape)
        exps = exps.astype(jnp.bfloat16)
        for k in range(count):
            mix = jnp.dot(
                exps[k * heads : (k + 1) * heads], values(k), preferred_element_type=jnp.float32
            )
            part_o[first + k] = jnp.where(upper, mix[:, :HEAD], mix[:, HEAD:])

    for copy in metas:
        copy.wait()
    spots = lax.broadcasted_iota(jnp.int32, table_v.shape, 0) * HEAD
    spots = spots + lax.broadcasted_iota(jnp.int32, table_v.shape, 1)
    table = jnp.full(table_v.shape, pages, jnp.int32)
    for page in range(pages):
        place = owner_ref[me * pages + page] * pages + slot_ref[me * pages + page]
        table = jnp.where(spots == place, page, table)
    table_v[...] = table
    table_copy = pltpu.make_async_copy(table_v, table_ref, meta_sem.at[3])
    table_copy.start()

    for j in range(seqs):
        q_wide[me * seqs + j] = widen(q_ref[j])
    part_o[pages] = jnp.zeros((heads, HEAD), jnp.float32)
    part_m[pages] = jnp.full((heads, HEAD), LOWEST, jnp.float32)
    part_l[pages] = jnp.zeros((heads, HEAD), jnp.float32)
    position = lax.broadcasted_iota(jnp.int32, (heads, resident), 1)
    scores = []
    for j in range(seqs):
        loads[j].wait()
        scores.append(
            jnp.where(
                position < length_ref[j],
                score(q_wide[me * seqs + j], cache_v[j, 0]),
                -jnp.inf,
            )
        )
    for load in loads[seqs + PAGE_PARTS :]:
        load.start()
    parts(seqs, scores, lambda j: cache_v[j, 1], pages + 1)

    for d in range(1, ranks):
        q_copies[d - 1].wait_recv()
        source = lax.rem(me - d + ranks, ranks)
        for j in range(seqs):
            q_wide[source * seqs + j] = widen(q_recv[d, j])

    for j in range(PAGE_PARTS):
        loads[seqs + j].wait()
        scores = []
        for page in range(j * step, (j + 1) * step):
            place = owner_ref[me * pages + page] * pages + slot_ref[me * pages + page]
            scores.append(score(q_wide[place // per_seq], pages_v[page, 0]))
        parts(step, scores, lambda k: pages_v[j * step + k, 1], j * step)
    table_copy.wait()

    lane = lax.broadcasted_iota(jnp.int32, (rows, HEAD), 1)
    row = lax.broadcasted_iota(jnp.int32, (rows, HEAD), 0)
    low_diagonal = lane == row
    high_diagonal = lane == row + rows

    def gather_owner(owner):
        peaks, totals, sums = [], [], []
        for j in range(seqs):
            spot = (owner * seqs + j) * per_seq
            slots = [table_ref[spot // HEAD, spot % HEAD + k] for k in range(per_seq)]
            slot_peaks = [part_m[slot] for slot in slots]
            peak = functools.reduce(jnp.maximum, slot_peaks)
            factors = [jnp.exp(one - peak) for one in slot_peaks]
            peaks.append(peak)
            totals.append(sum(f * part_l[slot] for f, slot in zip(factors, slots)))
            sums.append(sum(f * part_o[slot] for f, slot in zip(factors, slots)))
        return [jnp.concatenate(x, axis=0) for x in (peaks, totals, sums)]

    o_copies, ml_copies = [], []
    for d in range(1, ranks):
        peak, total, mix = gather_owner(lax.rem(me + d, ranks))
        o_send[d] = mix.astype(jnp.bfloat16)
        packed = jnp.where(low_diagonal, peak, jnp.where(high_diagonal, total, 0.0))
        ml_send[d] = jnp.broadcast_to(jnp.sum(packed, axis=0, keepdims=True), (8, HEAD))
        o_copies.append(to_rank(d, o_send.at[d], o_recv, o_sems))
        ml_copies.append(to_rank(d, ml_send.at[d], ml_recv, ml_sems))
        ml_copies[-1].start()
        o_copies[-1].start()

    peak, total, mix = gather_owner(me)
    own = pl.ds(pages + 1, seqs)
    states = [
        (peak, total, mix),
        tuple(x[own].reshape(rows, HEAD) for x in (part_m, part_l, part_o)),
    ]

    def merge(a, b):
        top = jnp.maximum(a[0], b[0])
        fa, fb = jnp.exp(a[0] - top), jnp.exp(b[0] - top)
        return top, fa * a[1] + fb * b[1], fa * a[2] + fb * b[2]

    state = merge(*states)
    for d in range(1, ranks):
        ml_copies[d - 1].wait_recv()
        o_copies[d - 1].wait_recv()
        spread = jnp.broadcast_to(ml_recv[d, 0:1, :], (rows, HEAD))
        peak = jnp.sum(jnp.where(low_diagonal, spread, 0.0), axis=1, keepdims=True)
        total = jnp.sum(jnp.where(high_diagonal, spread, 0.0), axis=1, keepdims=True)
        state = merge(
            state,
            (
                jnp.broadcast_to(peak, (rows, HEAD)),
                jnp.broadcast_to(total, (rows, HEAD)),
                o_recv[d].astype(jnp.float32),
            ),
        )
    attended = (state[2] / state[1]).astype(jnp.bfloat16)
    att_send[...] = attended
    att_copies = [to_rank(d, att_send, att_recv, att_sems) for d in range(1, ranks)]
    for copy in att_copies:
        copy.start()

    def place(source, value):
        att_f32[pl.ds(source * seqs, seqs)] = value.astype(jnp.float32).reshape(seqs, heads, HEAD)

    place(me, attended)
    for d in range(1, ranks):
        att_copies[d - 1].wait_recv()
        place(lax.rem(me - d + ranks, ranks), att_recv[d])
    for h in range(heads):
        att_wide[:, h * HEAD : (h + 1) * HEAD] = att_f32[:, h, :].astype(jnp.bfloat16)

    for j in range(W_PARTS):
        loads[seqs + PAGE_PARTS + j].wait()
    width = weight_v.shape[1]
    block = min(width, 512)
    share = all_seqs // tensors

    @pl.loop(0, width // block)
    def _(n):
        span = pl.ds(pl.multiple_of(n * block, block), block)
        product = jnp.dot(att_wide[...], weight_v[:, span], preferred_element_type=jnp.float32)
        for t in range(tensors):
            terms[t, :, span] = product[t * share : (t + 1) * share]

    _, sum_rows, sum_cols = sum_send.shape
    folds = sum_rows // share

    def fold(t):
        chunk = terms[t]
        return jnp.concatenate(
            [chunk[:, c * sum_cols : (c + 1) * sum_cols] for c in range(folds)], axis=0
        )

    sum_copies = []
    for d in range(1, tensors):
        target = lax.rem(my_tensor + d, tensors)
        sum_send[d] = fold(target).astype(jnp.bfloat16)
        copy = pltpu.make_async_remote_copy(
            src_ref=sum_send.at[d],
            dst_ref=sum_recv.at[d],
            send_sem=sum_sems.at[0, d],
            recv_sem=sum_sems.at[1, d],
            device_id={"tensor": target},
            device_id_type=MESH,
        )
        copy.start()
        sum_copies.append(copy)
    result = fold(my_tensor)
    for d in range(1, tensors):
        sum_copies[d - 1].wait_recv()
        result = result + sum_recv[d].astype(jnp.float32)
    for c in range(folds):
        out_ref[:, c * sum_cols : (c + 1) * sum_cols] = result[
            c * share : (c + 1) * share
        ].astype(jnp.bfloat16)

    for copy in q_copies + o_copies + ml_copies + att_copies + sum_copies:
        copy.wait_send()


def per_device(queries, cache, pages, page_owner, page_slot, lengths, out_weight):
    ranks = lax.axis_size("ranks")
    tensors = lax.axis_size("tensor")
    seqs, width = queries.shape
    heads = width // HEAD
    page_count = pages.shape[0]
    kv_width = cache.shape[-1]
    resident = cache.shape[2]
    features = out_weight.shape[1]
    all_seqs = ranks * seqs
    share = all_seqs // tensors
    folds = max(1, 16 // share)
    rows = seqs * heads
    slots = page_count + 1 + seqs
    table_shape = (pl.cdiv(ranks * page_count, HEAD), HEAD)
    bf16, f32 = jnp.bfloat16, jnp.float32
    vmem = pl.BlockSpec(memory_space=pltpu.VMEM)
    hbm = pl.BlockSpec(memory_space=pltpu.HBM)
    sems = pltpu.SemaphoreType.DMA
    return pl.pallas_call(
        functools.partial(kernel, ranks, tensors),
        out_shape=jax.ShapeDtypeStruct((share, features), bf16),
        in_specs=[hbm, hbm, hbm, vmem, hbm, hbm, hbm],
        out_specs=vmem,
        scratch_shapes=[
            pltpu.SMEM(page_owner.shape, jnp.int32),
            pltpu.SMEM(page_slot.shape, jnp.int32),
            pltpu.SMEM(lengths.shape, jnp.int32),
            pltpu.VMEM(table_shape, jnp.int32),
            pltpu.SMEM(table_shape, jnp.int32),
            pltpu.VMEM((seqs, heads, HEAD), f32),
            pltpu.VMEM((seqs, heads, HEAD), bf16),
            pltpu.VMEM(cache.shape, bf16),
            pltpu.VMEM(pages.shape, bf16),
            pltpu.VMEM(out_weight.shape, bf16),
            pltpu.VMEM((ranks, seqs, heads, HEAD), bf16),
            pltpu.VMEM((all_seqs, heads, kv_width), bf16),
            pltpu.VMEM((slots, heads, HEAD), f32),
            pltpu.VMEM((slots, heads, HEAD), f32),
            pltpu.VMEM((slots, heads, HEAD), f32),
            pltpu.VMEM((ranks, rows, HEAD), bf16),
            pltpu.VMEM((ranks, rows, HEAD), bf16),
            pltpu.VMEM((ranks, 8, HEAD), f32),
            pltpu.VMEM((ranks, 8, HEAD), f32),
            pltpu.VMEM((rows, HEAD), bf16),
            pltpu.VMEM((ranks, rows, HEAD), bf16),
            pltpu.VMEM((all_seqs, heads, HEAD), f32),
            pltpu.VMEM((all_seqs, width), bf16),
            pltpu.VMEM((tensors, share, features), f32),
            pltpu.VMEM((tensors, share * folds, features // folds), bf16),
            pltpu.VMEM((tensors, share * folds, features // folds), bf16),
            sems((4,)),
            sems((seqs + PAGE_PARTS + W_PARTS,)),
            sems((2, ranks)),
            sems((2, ranks)),
            sems((2, ranks)),
            sems((2, ranks)),
            sems((2, tensors)),
        ],
        compiler_params=pltpu.CompilerParams(
            collective_id=0, has_side_effects=True, vmem_limit_bytes=48 * 1024 * 1024
        ),
        cost_estimate=pl.CostEstimate(
            flops=2 * all_seqs * width * features,
            bytes_accessed=2 * (cache.size + pages.size + out_weight.size),
            transcendentals=0,
        ),
    )(
        page_owner,
        page_slot,
        lengths,
        queries,
        cache,
        pages,
        out_weight,
    )


def solution(mesh):
    placed = (
        P(("groups", "ranks"), "tensor"),
        P(("groups", "ranks"), None, None, "tensor"),
        P(("groups", "ranks"), None, None, "tensor"),
        P("groups"),
        P("groups"),
        P(("groups", "ranks")),
        P("tensor", "ranks"),
    )
    return jax.shard_map(
        per_device,
        mesh=mesh,
        in_specs=placed,
        out_specs=P(("groups", "tensor"), "ranks"),
        check_vma=False,
    )
```

```python
import functools

import jax
import jax.numpy as jnp
from jax import lax
from jax.experimental import pallas as pl
from jax.experimental.pallas import tpu as pltpu
from jax.sharding import PartitionSpec as P

HEAD = 128
MESH = pl.DeviceIdType.MESH
LOWEST = -1e30
W_PARTS = 4
PAGE_PARTS = 4


def kernel(
    ranks,
    tensors,
    owner_hbm,
    slot_hbm,
    length_hbm,
    query_ref,
    cache_hbm,
    pages_hbm,
    weight_hbm,
    out_ref,
    owner_ref,
    slot_ref,
    length_ref,
    table_v,
    table_ref,
    q_f32,
    q_ref,
    cache_v,
    pages_v,
    weight_v,
    q_recv,
    q_wide,
    part_o,
    part_m,
    part_l,
    o_send,
    o_recv,
    att_send,
    att_recv,
    att_f32,
    att_wide,
    terms,
    sum_send,
    sum_recv,
    meta_sem,
    load_sem,
    q_sems,
    o_sems,
    att_sems,
    sum_sems,
):
    me = lax.axis_index("ranks")
    my_tensor = lax.axis_index("tensor")
    seqs, heads, _ = q_ref.shape
    pages = pages_v.shape[0]
    per_seq = pages // seqs
    resident = cache_v.shape[2]
    half = heads // 2
    all_seqs = ranks * seqs
    scale = HEAD ** (-0.5)
    rows = seqs * heads

    metas = [
        pltpu.make_async_copy(source, target, meta_sem.at[k])
        for k, (source, target) in enumerate(
            ((owner_hbm, owner_ref), (slot_hbm, slot_ref), (length_hbm, length_ref))
        )
    ]
    for copy in metas:
        copy.start()

    loads = []
    for j in range(seqs):
        loads.append(pltpu.make_async_copy(cache_hbm.at[j], cache_v.at[j], load_sem.at[j]))
    step = pages // PAGE_PARTS
    for j in range(PAGE_PARTS):
        span = pl.ds(j * step, step)
        loads.append(
            pltpu.make_async_copy(pages_hbm.at[span], pages_v.at[span], load_sem.at[seqs + j])
        )
    depth = weight_v.shape[0] // W_PARTS
    for j in range(W_PARTS):
        span = pl.ds(j * depth, depth)
        loads.append(
            pltpu.make_async_copy(
                weight_hbm.at[span], weight_v.at[span], load_sem.at[seqs + PAGE_PARTS + j]
            )
        )
    for load in loads[: seqs + PAGE_PARTS]:
        load.start()

    barrier = pltpu.get_barrier_semaphore()
    for d in range(1, ranks):
        pl.semaphore_signal(
            barrier, inc=1, device_id={"ranks": lax.rem(me + d, ranks)}, device_id_type=MESH
        )
    for d in range(1, tensors):
        pl.semaphore_signal(
            barrier,
            inc=1,
            device_id={"tensor": lax.rem(my_tensor + d, tensors)},
            device_id_type=MESH,
        )
    for h in range(heads):
        q_f32[:, h, :] = query_ref[:, h * HEAD : (h + 1) * HEAD].astype(jnp.float32)
    q_ref[...] = q_f32[...].astype(jnp.bfloat16)
    pl.semaphore_wait(barrier, ranks + tensors - 2)

    def to_rank(d, source, target, sems):
        return pltpu.make_async_remote_copy(
            src_ref=source,
            dst_ref=target.at[d],
            send_sem=sems.at[0, d],
            recv_sem=sems.at[1, d],
            device_id={"ranks": lax.rem(me + d, ranks)},
            device_id_type=MESH,
        )

    q_copies = [to_rank(d, q_ref, q_recv, q_sems) for d in range(1, ranks)]
    for copy in q_copies:
        copy.start()

    upper = lax.broadcasted_iota(jnp.int32, (heads, HEAD), 0) < half

    def widen(q):
        wide = q.astype(jnp.float32)
        zero = jnp.zeros_like(wide)
        return jnp.concatenate(
            [jnp.where(upper, wide, zero), jnp.where(upper, zero, wide)], axis=1
        ).astype(jnp.bfloat16)

    def score(q, keys):
        return (
            lax.dot_general(q, keys, (((1,), (1,)), ((), ())), preferred_element_type=jnp.float32)
            * scale
        )

    def parts(count, scores, values, first):
        block = jnp.concatenate(scores, axis=0)
        peak = jnp.max(block, axis=1, keepdims=True)
        exps = jnp.exp(block - peak)
        total = jnp.sum(exps, axis=1, keepdims=True)
        span = pl.ds(first, count)
        shape = (count, heads, HEAD)
        part_m[span] = jnp.broadcast_to(peak, (count * heads, HEAD)).reshape(shape)
        part_l[span] = jnp.broadcast_to(total, (count * heads, HEAD)).reshape(shape)
        exps = exps.astype(jnp.bfloat16)
        for k in range(count):
            mix = jnp.dot(
                exps[k * heads : (k + 1) * heads], values(k), preferred_element_type=jnp.float32
            )
            part_o[first + k] = jnp.where(upper, mix[:, :HEAD], mix[:, HEAD:])

    for copy in metas:
        copy.wait()
    spots = lax.broadcasted_iota(jnp.int32, table_v.shape, 0) * HEAD
    spots = spots + lax.broadcasted_iota(jnp.int32, table_v.shape, 1)
    table = jnp.full(table_v.shape, pages, jnp.int32)
    for page in range(pages):
        place = owner_ref[me * pages + page] * pages + slot_ref[me * pages + page]
        table = jnp.where(spots == place, page, table)
    table_v[...] = table
    table_copy = pltpu.make_async_copy(table_v, table_ref, meta_sem.at[3])
    table_copy.start()

    for j in range(seqs):
        q_wide[me * seqs + j] = widen(q_ref[j])
    part_o[pages] = jnp.zeros((heads, HEAD), jnp.float32)
    part_m[pages] = jnp.full((heads, HEAD), LOWEST, jnp.float32)
    part_l[pages] = jnp.zeros((heads, HEAD), jnp.float32)
    position = lax.broadcasted_iota(jnp.int32, (heads, resident), 1)
    scores = []
    for j in range(seqs):
        loads[j].wait()
        scores.append(
            jnp.where(
                position < length_ref[j],
                score(q_wide[me * seqs + j], cache_v[j, 0]),
                -jnp.inf,
            )
        )
    for load in loads[seqs + PAGE_PARTS :]:
        load.start()
    parts(seqs, scores, lambda j: cache_v[j, 1], pages + 1)

    for d in range(1, ranks):
        q_copies[d - 1].wait_recv()
        source = lax.rem(me - d + ranks, ranks)
        for j in range(seqs):
            q_wide[source * seqs + j] = widen(q_recv[d, j])

    for j in range(PAGE_PARTS):
        loads[seqs + j].wait()
        scores = []
        for page in range(j * step, (j + 1) * step):
            place = owner_ref[me * pages + page] * pages + slot_ref[me * pages + page]
            scores.append(score(q_wide[place // per_seq], pages_v[page, 0]))
        parts(step, scores, lambda k: pages_v[j * step + k, 1], j * step)
    table_copy.wait()

    lane = lax.broadcasted_iota(jnp.int32, (rows, HEAD), 1)
    row = lax.broadcasted_iota(jnp.int32, (rows, HEAD), 0)
    low_diagonal = lane == row
    high_diagonal = lane == row + rows

    def gather_owner(owner):
        peaks, totals, sums = [], [], []
        for j in range(seqs):
            spot = (owner * seqs + j) * per_seq
            slots = [table_ref[spot // HEAD, spot % HEAD + k] for k in range(per_seq)]
            slot_peaks = [part_m[slot] for slot in slots]
            peak = functools.reduce(jnp.maximum, slot_peaks)
            factors = [jnp.exp(one - peak) for one in slot_peaks]
            peaks.append(peak)
            totals.append(sum(f * part_l[slot] for f, slot in zip(factors, slots)))
            sums.append(sum(f * part_o[slot] for f, slot in zip(factors, slots)))
        return [jnp.concatenate(x, axis=0) for x in (peaks, totals, sums)]

    third = lax.broadcasted_iota(jnp.int32, (16, HEAD), 0)

    def split(exact):
        high = exact.astype(jnp.bfloat16).astype(jnp.float32)
        rest = exact - high
        middle = rest.astype(jnp.bfloat16).astype(jnp.float32)
        low = rest - middle
        tile = jnp.where(third == 2, low, 0.0)
        tile = jnp.where(third == 1, middle, tile)
        return jnp.where(third == 0, high, tile).astype(jnp.bfloat16)

    o_copies = []
    for d in range(1, ranks):
        peak, total, mix = gather_owner(lax.rem(me + d, ranks))
        o_send[d, :rows] = mix.astype(jnp.bfloat16)
        packed = jnp.where(low_diagonal, peak, jnp.where(high_diagonal, total, 0.0))
        o_send[d, rows:] = split(jnp.sum(packed, axis=0, keepdims=True))
        o_copies.append(to_rank(d, o_send.at[d], o_recv, o_sems))
        o_copies[-1].start()

    peak, total, mix = gather_owner(me)
    own = pl.ds(pages + 1, seqs)
    states = [
        (peak, total, mix),
        tuple(x[own].reshape(rows, HEAD) for x in (part_m, part_l, part_o)),
    ]

    def merge(a, b):
        top = jnp.maximum(a[0], b[0])
        fa, fb = jnp.exp(a[0] - top), jnp.exp(b[0] - top)
        return top, fa * a[1] + fb * b[1], fa * a[2] + fb * b[2]

    state = merge(*states)
    for d in range(1, ranks):
        o_copies[d - 1].wait_recv()
        exact = jnp.sum(o_recv[d, rows:].astype(jnp.float32), axis=0, keepdims=True)
        spread = jnp.broadcast_to(exact, (rows, HEAD))
        peak = jnp.sum(jnp.where(low_diagonal, spread, 0.0), axis=1, keepdims=True)
        total = jnp.sum(jnp.where(high_diagonal, spread, 0.0), axis=1, keepdims=True)
        state = merge(
            state,
            (
                jnp.broadcast_to(peak, (rows, HEAD)),
                jnp.broadcast_to(total, (rows, HEAD)),
                o_recv[d, :rows].astype(jnp.float32),
            ),
        )
    attended = (state[2] / state[1]).astype(jnp.bfloat16)
    att_send[...] = attended
    att_copies = [to_rank(d, att_send, att_recv, att_sems) for d in range(1, ranks)]
    for copy in att_copies:
        copy.start()

    def place(source, value):
        att_f32[pl.ds(source * seqs, seqs)] = value.astype(jnp.float32).reshape(seqs, heads, HEAD)

    place(me, attended)
    for d in range(1, ranks):
        att_copies[d - 1].wait_recv()
        place(lax.rem(me - d + ranks, ranks), att_recv[d])
    for h in range(heads):
        att_wide[:, h * HEAD : (h + 1) * HEAD] = att_f32[:, h, :].astype(jnp.bfloat16)

    for j in range(W_PARTS):
        loads[seqs + PAGE_PARTS + j].wait()
    width = weight_v.shape[1]
    block = min(width, 512)
    share = all_seqs // tensors

    @pl.loop(0, width // block)
    def _(n):
        span = pl.ds(pl.multiple_of(n * block, block), block)
        product = jnp.dot(att_wide[...], weight_v[:, span], preferred_element_type=jnp.float32)
        for t in range(tensors):
            terms[t, :, span] = product[t * share : (t + 1) * share]

    _, sum_rows, sum_cols = sum_send.shape
    folds = sum_rows // share

    def fold(t):
        chunk = terms[t]
        return jnp.concatenate(
            [chunk[:, c * sum_cols : (c + 1) * sum_cols] for c in range(folds)], axis=0
        )

    sum_copies = []
    for d in range(1, tensors):
        target = lax.rem(my_tensor + d, tensors)
        sum_send[d] = fold(target).astype(jnp.bfloat16)
        copy = pltpu.make_async_remote_copy(
            src_ref=sum_send.at[d],
            dst_ref=sum_recv.at[d],
            send_sem=sum_sems.at[0, d],
            recv_sem=sum_sems.at[1, d],
            device_id={"tensor": target},
            device_id_type=MESH,
        )
        copy.start()
        sum_copies.append(copy)
    result = fold(my_tensor)
    for d in range(1, tensors):
        sum_copies[d - 1].wait_recv()
        result = result + sum_recv[d].astype(jnp.float32)
    for c in range(folds):
        out_ref[:, c * sum_cols : (c + 1) * sum_cols] = result[
            c * share : (c + 1) * share
        ].astype(jnp.bfloat16)

    for copy in q_copies + o_copies + att_copies + sum_copies:
        copy.wait_send()


def per_device(queries, cache, pages, page_owner, page_slot, lengths, out_weight):
    ranks = lax.axis_size("ranks")
    tensors = lax.axis_size("tensor")
    seqs, width = queries.shape
    heads = width // HEAD
    page_count = pages.shape[0]
    kv_width = cache.shape[-1]
    resident = cache.shape[2]
    features = out_weight.shape[1]
    all_seqs = ranks * seqs
    share = all_seqs // tensors
    folds = max(1, 16 // share)
    rows = seqs * heads
    slots = page_count + 1 + seqs
    table_shape = (pl.cdiv(ranks * page_count, HEAD), HEAD)
    bf16, f32 = jnp.bfloat16, jnp.float32
    vmem = pl.BlockSpec(memory_space=pltpu.VMEM)
    hbm = pl.BlockSpec(memory_space=pltpu.HBM)
    sems = pltpu.SemaphoreType.DMA
    return pl.pallas_call(
        functools.partial(kernel, ranks, tensors),
        out_shape=jax.ShapeDtypeStruct((share, features), bf16),
        in_specs=[hbm, hbm, hbm, vmem, hbm, hbm, hbm],
        out_specs=vmem,
        scratch_shapes=[
            pltpu.SMEM(page_owner.shape, jnp.int32),
            pltpu.SMEM(page_slot.shape, jnp.int32),
            pltpu.SMEM(lengths.shape, jnp.int32),
            pltpu.VMEM(table_shape, jnp.int32),
            pltpu.SMEM(table_shape, jnp.int32),
            pltpu.VMEM((seqs, heads, HEAD), f32),
            pltpu.VMEM((seqs, heads, HEAD), bf16),
            pltpu.VMEM(cache.shape, bf16),
            pltpu.VMEM(pages.shape, bf16),
            pltpu.VMEM(out_weight.shape, bf16),
            pltpu.VMEM((ranks, seqs, heads, HEAD), bf16),
            pltpu.VMEM((all_seqs, heads, kv_width), bf16),
            pltpu.VMEM((slots, heads, HEAD), f32),
            pltpu.VMEM((slots, heads, HEAD), f32),
            pltpu.VMEM((slots, heads, HEAD), f32),
            pltpu.VMEM((ranks, rows + 16, HEAD), bf16),
            pltpu.VMEM((ranks, rows + 16, HEAD), bf16),
            pltpu.VMEM((rows, HEAD), bf16),
            pltpu.VMEM((ranks, rows, HEAD), bf16),
            pltpu.VMEM((all_seqs, heads, HEAD), f32),
            pltpu.VMEM((all_seqs, width), bf16),
            pltpu.VMEM((tensors, share, features), f32),
            pltpu.VMEM((tensors, share * folds, features // folds), bf16),
            pltpu.VMEM((tensors, share * folds, features // folds), bf16),
            sems((4,)),
            sems((seqs + PAGE_PARTS + W_PARTS,)),
            sems((2, ranks)),
            sems((2, ranks)),
            sems((2, ranks)),
            sems((2, tensors)),
        ],
        compiler_params=pltpu.CompilerParams(
            collective_id=0, has_side_effects=True, vmem_limit_bytes=48 * 1024 * 1024
        ),
        cost_estimate=pl.CostEstimate(
            flops=2 * all_seqs * width * features,
            bytes_accessed=2 * (cache.size + pages.size + out_weight.size),
            transcendentals=0,
        ),
    )(
        page_owner,
        page_slot,
        lengths,
        queries,
        cache,
        pages,
        out_weight,
    )


def solution(mesh):
    placed = (
        P(("groups", "ranks"), "tensor"),
        P(("groups", "ranks"), None, None, "tensor"),
        P(("groups", "ranks"), None, None, "tensor"),
        P("groups"),
        P("groups"),
        P(("groups", "ranks")),
        P("tensor", "ranks"),
    )
    return jax.shard_map(
        per_device,
        mesh=mesh,
        in_specs=placed,
        out_specs=P(("groups", "tensor"), "ranks"),
        check_vma=False,
    )
```

```python
import functools

import jax
import jax.numpy as jnp
from jax import lax
from jax.experimental import pallas as pl
from jax.experimental.pallas import tpu as pltpu
from jax.sharding import PartitionSpec as P

HEAD = 128
MESH = pl.DeviceIdType.MESH
LOWEST = -1e30
W_PARTS = 4
PAGE_PARTS = 1


def kernel(
    ranks,
    tensors,
    owner_hbm,
    slot_hbm,
    length_hbm,
    query_ref,
    cache_hbm,
    pages_hbm,
    weight_hbm,
    out_ref,
    owner_ref,
    slot_ref,
    length_ref,
    table_v,
    table_ref,
    q_f32,
    q_ref,
    cache_v,
    pages_v,
    weight_v,
    q_recv,
    q_wide,
    part_o,
    part_m,
    part_l,
    o_send,
    o_recv,
    att_send,
    att_recv,
    att_f32,
    att_wide,
    terms,
    sum_send,
    sum_recv,
    meta_sem,
    load_sem,
    q_sems,
    o_sems,
    att_sems,
    sum_sems,
):
    me = lax.axis_index("ranks")
    my_tensor = lax.axis_index("tensor")
    seqs, heads, _ = q_ref.shape
    pages = pages_v.shape[0]
    per_seq = pages // seqs
    resident = cache_v.shape[2]
    half = heads // 2
    all_seqs = ranks * seqs
    scale = HEAD ** (-0.5)
    rows = seqs * heads

    metas = [
        pltpu.make_async_copy(source, target, meta_sem.at[k])
        for k, (source, target) in enumerate(
            ((owner_hbm, owner_ref), (slot_hbm, slot_ref), (length_hbm, length_ref))
        )
    ]
    for copy in metas:
        copy.start()

    loads = []
    for j in range(seqs):
        loads.append(pltpu.make_async_copy(cache_hbm.at[j], cache_v.at[j], load_sem.at[j]))
    step = pages // PAGE_PARTS
    for j in range(PAGE_PARTS):
        span = pl.ds(j * step, step)
        loads.append(
            pltpu.make_async_copy(pages_hbm.at[span], pages_v.at[span], load_sem.at[seqs + j])
        )
    depth = weight_v.shape[0] // W_PARTS
    for j in range(W_PARTS):
        span = pl.ds(j * depth, depth)
        loads.append(
            pltpu.make_async_copy(
                weight_hbm.at[span], weight_v.at[span], load_sem.at[seqs + PAGE_PARTS + j]
            )
        )
    for load in loads[: seqs + PAGE_PARTS]:
        load.start()

    barrier = pltpu.get_barrier_semaphore()
    for d in range(1, ranks):
        pl.semaphore_signal(
            barrier, inc=1, device_id={"ranks": lax.rem(me + d, ranks)}, device_id_type=MESH
        )
    for d in range(1, tensors):
        pl.semaphore_signal(
            barrier,
            inc=1,
            device_id={"tensor": lax.rem(my_tensor + d, tensors)},
            device_id_type=MESH,
        )
    for h in range(heads):
        q_f32[:, h, :] = query_ref[:, h * HEAD : (h + 1) * HEAD].astype(jnp.float32)
    q_ref[...] = q_f32[...].astype(jnp.bfloat16)
    pl.semaphore_wait(barrier, ranks + tensors - 2)

    def to_rank(d, source, target, sems):
        return pltpu.make_async_remote_copy(
            src_ref=source,
            dst_ref=target.at[d],
            send_sem=sems.at[0, d],
            recv_sem=sems.at[1, d],
            device_id={"ranks": lax.rem(me + d, ranks)},
            device_id_type=MESH,
        )

    q_copies = [to_rank(d, q_ref, q_recv, q_sems) for d in range(1, ranks)]
    for copy in q_copies:
        copy.start()

    upper = lax.broadcasted_iota(jnp.int32, (heads, HEAD), 0) < half

    def widen(q):
        wide = q.astype(jnp.float32)
        zero = jnp.zeros_like(wide)
        return jnp.concatenate(
            [jnp.where(upper, wide, zero), jnp.where(upper, zero, wide)], axis=1
        ).astype(jnp.bfloat16)

    def score(q, keys):
        return (
            lax.dot_general(q, keys, (((1,), (1,)), ((), ())), preferred_element_type=jnp.float32)
            * scale
        )

    def parts(count, scores, values, first):
        block = jnp.concatenate(scores, axis=0)
        peak = jnp.max(block, axis=1, keepdims=True)
        exps = jnp.exp(block - peak)
        total = jnp.sum(exps, axis=1, keepdims=True)
        span = pl.ds(first, count)
        shape = (count, heads, HEAD)
        part_m[span] = jnp.broadcast_to(peak, (count * heads, HEAD)).reshape(shape)
        part_l[span] = jnp.broadcast_to(total, (count * heads, HEAD)).reshape(shape)
        exps = exps.astype(jnp.bfloat16)
        for k in range(count):
            mix = jnp.dot(
                exps[k * heads : (k + 1) * heads], values(k), preferred_element_type=jnp.float32
            )
            part_o[first + k] = jnp.where(upper, mix[:, :HEAD], mix[:, HEAD:])

    for copy in metas:
        copy.wait()
    spots = lax.broadcasted_iota(jnp.int32, table_v.shape, 0) * HEAD
    spots = spots + lax.broadcasted_iota(jnp.int32, table_v.shape, 1)
    table = jnp.full(table_v.shape, pages, jnp.int32)
    for page in range(pages):
        place = owner_ref[me * pages + page] * pages + slot_ref[me * pages + page]
        table = jnp.where(spots == place, page, table)
    table_v[...] = table
    table_copy = pltpu.make_async_copy(table_v, table_ref, meta_sem.at[3])
    table_copy.start()

    for j in range(seqs):
        q_wide[me * seqs + j] = widen(q_ref[j])
    part_o[pages] = jnp.zeros((heads, HEAD), jnp.float32)
    part_m[pages] = jnp.full((heads, HEAD), LOWEST, jnp.float32)
    part_l[pages] = jnp.zeros((heads, HEAD), jnp.float32)
    position = lax.broadcasted_iota(jnp.int32, (heads, resident), 1)
    scores = []
    for j in range(seqs):
        loads[j].wait()
        scores.append(
            jnp.where(
                position < length_ref[j],
                score(q_wide[me * seqs + j], cache_v[j, 0]),
                -jnp.inf,
            )
        )
    for load in loads[seqs + PAGE_PARTS :]:
        load.start()
    parts(seqs, scores, lambda j: cache_v[j, 1], pages + 1)

    for d in range(1, ranks):
        q_copies[d - 1].wait_recv()
        source = lax.rem(me - d + ranks, ranks)
        for j in range(seqs):
            q_wide[source * seqs + j] = widen(q_recv[d, j])

    for j in range(PAGE_PARTS):
        loads[seqs + j].wait()
        scores = []
        for page in range(j * step, (j + 1) * step):
            place = owner_ref[me * pages + page] * pages + slot_ref[me * pages + page]
            scores.append(score(q_wide[place // per_seq], pages_v[page, 0]))
        parts(step, scores, lambda k: pages_v[j * step + k, 1], j * step)
    table_copy.wait()

    lane = lax.broadcasted_iota(jnp.int32, (rows, HEAD), 1)
    row = lax.broadcasted_iota(jnp.int32, (rows, HEAD), 0)
    low_diagonal = lane == row
    high_diagonal = lane == row + rows

    def gather_owner(owner):
        peaks, totals, sums = [], [], []
        for j in range(seqs):
            spot = (owner * seqs + j) * per_seq
            slots = [table_ref[spot // HEAD, spot % HEAD + k] for k in range(per_seq)]
            slot_peaks = [part_m[slot] for slot in slots]
            peak = functools.reduce(jnp.maximum, slot_peaks)
            factors = [jnp.exp(one - peak) for one in slot_peaks]
            peaks.append(peak)
            totals.append(sum(f * part_l[slot] for f, slot in zip(factors, slots)))
            sums.append(sum(f * part_o[slot] for f, slot in zip(factors, slots)))
        return [jnp.concatenate(x, axis=0) for x in (peaks, totals, sums)]

    third = lax.broadcasted_iota(jnp.int32, (16, HEAD), 0)

    def split(exact):
        high = exact.astype(jnp.bfloat16).astype(jnp.float32)
        rest = exact - high
        middle = rest.astype(jnp.bfloat16).astype(jnp.float32)
        low = rest - middle
        tile = jnp.where(third == 2, low, 0.0)
        tile = jnp.where(third == 1, middle, tile)
        return jnp.where(third == 0, high, tile).astype(jnp.bfloat16)

    o_copies = []
    for d in range(1, ranks):
        peak, total, mix = gather_owner(lax.rem(me + d, ranks))
        o_send[d, :rows] = mix.astype(jnp.bfloat16)
        packed = jnp.where(low_diagonal, peak, jnp.where(high_diagonal, total, 0.0))
        o_send[d, rows:] = split(jnp.sum(packed, axis=0, keepdims=True))
        o_copies.append(to_rank(d, o_send.at[d], o_recv, o_sems))
        o_copies[-1].start()

    peak, total, mix = gather_owner(me)
    own = pl.ds(pages + 1, seqs)
    states = [
        (peak, total, mix),
        tuple(x[own].reshape(rows, HEAD) for x in (part_m, part_l, part_o)),
    ]

    def merge(a, b):
        top = jnp.maximum(a[0], b[0])
        fa, fb = jnp.exp(a[0] - top), jnp.exp(b[0] - top)
        return top, fa * a[1] + fb * b[1], fa * a[2] + fb * b[2]

    state = merge(*states)
    for d in range(1, ranks):
        o_copies[d - 1].wait_recv()
        exact = jnp.sum(o_recv[d, rows:].astype(jnp.float32), axis=0, keepdims=True)
        spread = jnp.broadcast_to(exact, (rows, HEAD))
        peak = jnp.sum(jnp.where(low_diagonal, spread, 0.0), axis=1, keepdims=True)
        total = jnp.sum(jnp.where(high_diagonal, spread, 0.0), axis=1, keepdims=True)
        state = merge(
            state,
            (
                jnp.broadcast_to(peak, (rows, HEAD)),
                jnp.broadcast_to(total, (rows, HEAD)),
                o_recv[d, :rows].astype(jnp.float32),
            ),
        )
    attended = (state[2] / state[1]).astype(jnp.bfloat16)
    att_send[...] = attended
    att_copies = [to_rank(d, att_send, att_recv, att_sems) for d in range(1, ranks)]
    for copy in att_copies:
        copy.start()

    def place(source, value):
        att_f32[pl.ds(source * seqs, seqs)] = value.astype(jnp.float32).reshape(seqs, heads, HEAD)

    place(me, attended)
    for d in range(1, ranks):
        att_copies[d - 1].wait_recv()
        place(lax.rem(me - d + ranks, ranks), att_recv[d])
    for h in range(heads):
        att_wide[:, h * HEAD : (h + 1) * HEAD] = att_f32[:, h, :].astype(jnp.bfloat16)

    for j in range(W_PARTS):
        loads[seqs + PAGE_PARTS + j].wait()
    width = weight_v.shape[1]
    block = min(width, 1024)
    share = all_seqs // tensors

    @pl.loop(0, width // block)
    def _(n):
        span = pl.ds(pl.multiple_of(n * block, block), block)
        product = jnp.dot(att_wide[...], weight_v[:, span], preferred_element_type=jnp.float32)
        for t in range(tensors):
            terms[t, :, span] = product[t * share : (t + 1) * share]

    _, sum_rows, sum_cols = sum_send.shape
    folds = sum_rows // share

    def fold(t):
        chunk = terms[t]
        return jnp.concatenate(
            [chunk[:, c * sum_cols : (c + 1) * sum_cols] for c in range(folds)], axis=0
        )

    sum_copies = []
    for d in range(1, tensors):
        target = lax.rem(my_tensor + d, tensors)
        sum_send[d] = fold(target).astype(jnp.bfloat16)
        copy = pltpu.make_async_remote_copy(
            src_ref=sum_send.at[d],
            dst_ref=sum_recv.at[d],
            send_sem=sum_sems.at[0, d],
            recv_sem=sum_sems.at[1, d],
            device_id={"tensor": target},
            device_id_type=MESH,
        )
        copy.start()
        sum_copies.append(copy)
    result = fold(my_tensor)
    for d in range(1, tensors):
        sum_copies[d - 1].wait_recv()
        result = result + sum_recv[d].astype(jnp.float32)
    for c in range(folds):
        out_ref[:, c * sum_cols : (c + 1) * sum_cols] = result[
            c * share : (c + 1) * share
        ].astype(jnp.bfloat16)

    for copy in q_copies + o_copies + att_copies + sum_copies:
        copy.wait_send()


def per_device(queries, cache, pages, page_owner, page_slot, lengths, out_weight):
    ranks = lax.axis_size("ranks")
    tensors = lax.axis_size("tensor")
    seqs, width = queries.shape
    heads = width // HEAD
    page_count = pages.shape[0]
    kv_width = cache.shape[-1]
    resident = cache.shape[2]
    features = out_weight.shape[1]
    all_seqs = ranks * seqs
    share = all_seqs // tensors
    folds = max(1, 16 // share)
    rows = seqs * heads
    slots = page_count + 1 + seqs
    table_shape = (pl.cdiv(ranks * page_count, HEAD), HEAD)
    bf16, f32 = jnp.bfloat16, jnp.float32
    vmem = pl.BlockSpec(memory_space=pltpu.VMEM)
    hbm = pl.BlockSpec(memory_space=pltpu.HBM)
    sems = pltpu.SemaphoreType.DMA
    return pl.pallas_call(
        functools.partial(kernel, ranks, tensors),
        out_shape=jax.ShapeDtypeStruct((share, features), bf16),
        in_specs=[hbm, hbm, hbm, vmem, hbm, hbm, hbm],
        out_specs=vmem,
        scratch_shapes=[
            pltpu.SMEM(page_owner.shape, jnp.int32),
            pltpu.SMEM(page_slot.shape, jnp.int32),
            pltpu.SMEM(lengths.shape, jnp.int32),
            pltpu.VMEM(table_shape, jnp.int32),
            pltpu.SMEM(table_shape, jnp.int32),
            pltpu.VMEM((seqs, heads, HEAD), f32),
            pltpu.VMEM((seqs, heads, HEAD), bf16),
            pltpu.VMEM(cache.shape, bf16),
            pltpu.VMEM(pages.shape, bf16),
            pltpu.VMEM(out_weight.shape, bf16),
            pltpu.VMEM((ranks, seqs, heads, HEAD), bf16),
            pltpu.VMEM((all_seqs, heads, kv_width), bf16),
            pltpu.VMEM((slots, heads, HEAD), f32),
            pltpu.VMEM((slots, heads, HEAD), f32),
            pltpu.VMEM((slots, heads, HEAD), f32),
            pltpu.VMEM((ranks, rows + 16, HEAD), bf16),
            pltpu.VMEM((ranks, rows + 16, HEAD), bf16),
            pltpu.VMEM((rows, HEAD), bf16),
            pltpu.VMEM((ranks, rows, HEAD), bf16),
            pltpu.VMEM((all_seqs, heads, HEAD), f32),
            pltpu.VMEM((all_seqs, width), bf16),
            pltpu.VMEM((tensors, share, features), f32),
            pltpu.VMEM((tensors, share * folds, features // folds), bf16),
            pltpu.VMEM((tensors, share * folds, features // folds), bf16),
            sems((4,)),
            sems((seqs + PAGE_PARTS + W_PARTS,)),
            sems((2, ranks)),
            sems((2, ranks)),
            sems((2, ranks)),
            sems((2, tensors)),
        ],
        compiler_params=pltpu.CompilerParams(
            collective_id=0, has_side_effects=True, vmem_limit_bytes=48 * 1024 * 1024
        ),
        cost_estimate=pl.CostEstimate(
            flops=2 * all_seqs * width * features,
            bytes_accessed=2 * (cache.size + pages.size + out_weight.size),
            transcendentals=0,
        ),
    )(
        page_owner,
        page_slot,
        lengths,
        queries,
        cache,
        pages,
        out_weight,
    )


def solution(mesh):
    placed = (
        P(("groups", "ranks"), "tensor"),
        P(("groups", "ranks"), None, None, "tensor"),
        P(("groups", "ranks"), None, None, "tensor"),
        P("groups"),
        P("groups"),
        P(("groups", "ranks")),
        P("tensor", "ranks"),
    )
    return jax.shard_map(
        per_device,
        mesh=mesh,
        in_specs=placed,
        out_specs=P(("groups", "tensor"), "ranks"),
        check_vma=False,
    )
```
